128 devices in a mesh: patch: 64 (over y, z_hi, x, core), chan: 2 (over z_lo).
Axes of the slice: x: 4, y: 4, z: 4 (z_hi: 2, z_lo: 2; z = z_hi * 2 + z_lo), core: 2. Of those that a mesh axis runs over, the one named last changes fastest.
Arguments:
- coarse_map: bfloat16 [131072, 256], P('patch', 'chan'), may hold values from -6 to 6
- skip_map: bfloat16 [524288, 256], P('patch', 'chan'), may hold values from -6 to 6
- coarse_values: bfloat16 [131072, 576], P('patch'), may hold values from -0.125 to 0.125
- coarse_columns: int32 [2048, 9], P('patch'), may hold values from 0 to 2047, as said below
- fine_values: bfloat16 [524288, 576], P('patch'), may hold values from -0.125 to 0.125
- fine_columns: int32 [8192, 9], P('patch'), may hold values from 0 to 8191, as said below
- coarse_weight: bfloat16 [4, 256, 256], P(None, 'chan'), may hold values from -0.1875 to 0.1875
- coarse_bias: float32 [256], P('chan'), may hold values from -3 to 3
- up_weight: bfloat16 [4, 256, 256], P(None, 'chan'), may hold values from -0.125 to 0.125
- skip_weight: bfloat16 [4, 256, 256], P(None, 'chan'), may hold values from -0.125 to 0.125
- fine_bias: float32 [256], P('chan'), may hold values from -3 to 3
Outputs:
- restored: bfloat16 [524288, 256], P('patch', 'chan')
The draws below stay inside these ranges and needn't reach their ends.
Inputs may be any that keep to these rules, and one draw needn't show every extreme that they name: `coarse_columns`: each row r holds 9 distinct block indices of 0 to 2047, one of them r itself; each differs from r, cyclically modulo 2048, by at most 8, and that distance is reached. `fine_columns`: each row r holds 9 distinct block indices of 0 to 8191, one of them r itself; each differs from r, cyclically modulo 8192, by at most 16, and that distance is reached.
All inputs are finite; a program needn't handle non-finite values.
Results may differ from the reference program's by a relative error of at most 0.011.
Values may be sent and summed in bfloat16 or wider, within the bound.
A program may use at most 192 MiB of HBM per device.

```python
import jax
import jax.numpy as jnp
from jax import lax

B = 64
NB = 9
RIM_C = 8
TERMS = 4
CH = 256
CB = 32
RIM_F = 16
BC = 2048
BF = 8192
PC = 131072
PF = 524288
N_PATCH = 64


def draw_columns(key, block_total, per_device, reach_blocks, per_row):
    row_ids = jnp.arange(block_total, dtype=jnp.int32)
    position = row_ids % per_device
    forced = jnp.where(position < per_device // 2, -reach_blocks, reach_blocks).astype(jnp.int32)
    candidate = jnp.concatenate([jnp.arange(-reach_blocks, 0, dtype=jnp.int32), jnp.arange(1, reach_blocks + 1, dtype=jnp.int32)])
    key_pick, key_order = jax.random.split(key)
    scores = jax.random.randint(key_pick, (block_total, 2 * reach_blocks), 0, 2 ** 20, dtype=jnp.int32) * (2 * reach_blocks) + jnp.arange(2 * reach_blocks, dtype=jnp.int32)[None, :]
    scores = jnp.where(candidate[None, :] == forced[:, None], 2 ** 30, scores)
    chosen = jnp.argsort(scores, axis=1)[:, :per_row - 2]
    extra_ids = candidate[chosen]
    offsets = jnp.concatenate([jnp.zeros((block_total, 1), jnp.int32), forced[:, None], extra_ids], axis=1)
    shuffle_scores = jax.random.randint(key_order, (block_total, per_row), 0, 2 ** 20, dtype=jnp.int32) * per_row + jnp.arange(per_row, dtype=jnp.int32)[None, :]
    order_ids = jnp.argsort(shuffle_scores, axis=1)
    offsets = jnp.take_along_axis(offsets, order_ids, axis=1)
    return (row_ids[:, None] + offsets) % block_total


def draw_coarse_columns(key, part):
    key = jax.random.fold_in(key, 11)
    return draw_columns(key, BC, CB, RIM_C, NB)


def draw_fine_columns(key, part):
    key = jax.random.fold_in(key, 23)
    return draw_columns(key, BF, 4 * CB, RIM_F, NB)


def block_levels(rng, dims, pieces, low, largest):
    loudness = 1.0
    for dim, parts in pieces:
        draws = jax.random.uniform(jax.random.fold_in(jax.random.fold_in(rng, 6), dim), (parts,), jnp.float32, low / len(pieces), largest / len(pieces))
        loudness = loudness * jnp.repeat(jnp.exp(draws), dims[dim] // parts).reshape((-1,) + (1,) * (len(dims) - 1 - dim))
    return loudness


def gaussian(own_key, shape, deviation, reach, cuts=(), kind=jnp.bfloat16):
    values = deviation * jax.random.normal(own_key, shape, jnp.float32)
    if cuts:
        values = values * block_levels(own_key, shape, cuts, -0.22, 0.18)
    return jnp.clip(values, -reach, reach).astype(kind)


def setup_inputs(seed: int = 0) -> dict:
    arg_keys = jax.random.split(jax.random.key(seed), 12)
    coarse_map = gaussian(arg_keys[0], (PC, CH), 1.0, 6.0, ((0, 64), (1, 2)))
    skip_map = gaussian(arg_keys[1], (PF, CH), 1.0, 6.0, ((0, 64), (1, 2)))
    coarse_values = gaussian(arg_keys[2], (PC, NB * B), (4 * NB * B) ** -0.5, 0.125, ((0, 64),))
    coarse_columns = draw_coarse_columns(jax.random.fold_in(arg_keys[11], 71), 0)
    fine_values = gaussian(arg_keys[4], (PF, NB * B), (4 * NB * B) ** -0.5, 0.125, ((0, 64),))
    fine_columns = draw_fine_columns(jax.random.fold_in(arg_keys[11], 71), 0)
    coarse_weight = gaussian(arg_keys[6], (TERMS, CH, CH), (TERMS * CH) ** -0.5, 0.1875, ((1, 2),))
    coarse_bias = gaussian(arg_keys[7], (CH,), 0.5, 3.0, ((0, 2),), jnp.float32)
    up_weight = gaussian(arg_keys[8], (TERMS, CH, CH), (2 * TERMS * CH) ** -0.5, 0.125, ((1, 2),))
    skip_weight = gaussian(arg_keys[9], (TERMS, CH, CH), (2 * TERMS * CH) ** -0.5, 0.125, ((1, 2),))
    fine_bias = gaussian(arg_keys[10], (CH,), 0.5, 3.0, ((0, 2),), jnp.float32)
    return dict(coarse_map=coarse_map, skip_map=skip_map, coarse_values=coarse_values, coarse_columns=coarse_columns, fine_values=fine_values, fine_columns=fine_columns, coarse_weight=coarse_weight, coarse_bias=coarse_bias, up_weight=up_weight, skip_weight=skip_weight, fine_bias=fine_bias)


def apply_blocks(signal, entries, columns):
    channels = signal.shape[1]
    blocks = signal.reshape(-1, B, channels)
    group = columns.shape[0] // N_PATCH
    entry_groups = entries.reshape(N_PATCH, group, B, NB * B)
    column_groups = columns.reshape(N_PATCH, group, NB)

    def one_group(pair):
        entry_part, column_part = pair
        picked = blocks[column_part].reshape(group, NB * B, channels)
        return jnp.einsum("rpq,rqc->rpc", entry_part.astype(jnp.float32), picked.astype(jnp.float32))

    result = lax.map(one_group, (entry_groups, column_groups))
    return result.reshape(-1, channels)


def chebyshev(signal, entries, columns):
    series = [signal]
    series.append(apply_blocks(signal, entries, columns).astype(jnp.bfloat16))
    for order in range(2, TERMS):
        newer = 2.0 * apply_blocks(series[-1], entries, columns) - series[-2].astype(jnp.float32)
        series.append(newer.astype(jnp.bfloat16))
    return series


def reference(coarse_map, skip_map, coarse_values, coarse_columns, fine_values, fine_columns, coarse_weight, coarse_bias, up_weight, skip_weight, fine_bias):
    coarse_series = chebyshev(coarse_map, coarse_values, coarse_columns)
    summed = jnp.dot(coarse_series[0], coarse_weight[0], preferred_element_type=jnp.float32)
    for order in range(1, TERMS):
        summed = summed + jnp.dot(coarse_series[order], coarse_weight[order], preferred_element_type=jnp.float32)
    hidden = jnp.maximum(summed + coarse_bias, 0.0).astype(jnp.bfloat16)
    joined = jnp.concatenate([jnp.repeat(hidden, 4, axis=0), skip_map], axis=1)
    fine_series = chebyshev(joined, fine_values, fine_columns)
    result = jnp.zeros((joined.shape[0], CH), jnp.float32)
    for order in range(TERMS):
        result = result + jnp.dot(fine_series[order][:, :CH], up_weight[order], preferred_element_type=jnp.float32)
        result = result + jnp.dot(fine_series[order][:, CH:], skip_weight[order], preferred_element_type=jnp.float32)
    return (result + fine_bias).astype(jnp.bfloat16)
```

```python
import functools

import jax
import jax.numpy as jnp
from jax import lax
from jax.experimental import pallas as pl
from jax.experimental.pallas import tpu as pltpu
from jax.sharding import PartitionSpec as P

B = 64
NB = 9
RIM_C = 8
RIM_F = 16
TERMS = 4
FLIP = 8
F32 = jnp.float32
BF16 = jnp.bfloat16
MESH = pl.DeviceIdType.MESH


def dot(a, b):
    return jnp.dot(a, b, preferred_element_type=F32)


def place_of(offset, blocks_all, held):
    return jnp.minimum(lax.bitwise_and(offset, blocks_all - 1), held - 1)


def kernel(
    n_patch,
    cm,
    skip,
    vc_hbm,
    jc,
    vf_hbm,
    jf,
    wc_hbm,
    cb_hbm,
    up_hbm,
    sw_hbm,
    fb,
    out_hbm,
    cm_own,
    cm_oth,
    vc,
    wc,
    cb,
    up,
    sw,
    skip_own,
    skip_oth,
    vf,
    ce3,
    ce2,
    ce1,
    gc,
    hidden,
    g,
    b3,
    b2,
    b1,
    lo3,
    lo2,
    lo1,
    hi3,
    hi2,
    hi1,
    out,
    vct,
    vft,
    load_sem,
    vf_sem,
    gather_sem,
    skip_sem,
    halo_c_sem,
    halo_f_sem,
    out_sem,
):
    p = lax.axis_index("patch")
    c = lax.axis_index("chan")
    left = (lax.rem(p + n_patch - 1, n_patch), c)
    right = (lax.rem(p + 1, n_patch), c)
    partner = (p, 1 - c)
    z_hi = lax.rem(p // FLIP, 2)
    far = (p + FLIP - 2 * FLIP * z_hi, 1 - c)

    n_c = vc.shape[0]
    n_f = vf.shape[0]
    all_c = n_c * n_patch
    all_f = n_f * n_patch
    half = cm.shape[1]
    full = 2 * half

    def remote(src, dst, sems, target):
        return pltpu.make_async_remote_copy(
            src_ref=src,
            dst_ref=dst,
            send_sem=sems.at[0],
            recv_sem=sems.at[1],
            device_id=target,
            device_id_type=MESH,
        )

    own_rows = pl.ds(pl.multiple_of(c * half, half), half)
    own_cols = own_rows
    far_cols = pl.ds(pl.multiple_of((1 - c) * half, half), half)

    pairs = [
        (cm, cm_own),
        (wc_hbm, wc.at[:, pl.ds(0, half), :]),
        (cb_hbm, cb.at[c]),
        (vc_hbm, vct),
        (up_hbm.at[:, :, own_cols], up.at[:, own_rows, :]),
        (sw_hbm.at[:, :, own_cols], sw.at[:, pl.ds(0, half), :]),
        (skip, skip_own),
    ]
    loads = [pltpu.make_async_copy(a, b, load_sem.at[i]) for i, (a, b) in enumerate(pairs)]
    for load in loads:
        load.start()

    lanes = 128
    v_cols = vft.shape[2]
    v_parts = n_f * B // v_cols

    def vf_load(i, slot):
        cols = pl.ds(pl.multiple_of(i * v_cols, v_cols), v_cols)
        return pltpu.make_async_copy(vf_hbm.at[:, cols], vft.at[slot], vf_sem.at[slot])

    vf_load(0, 0).start()
    vf_load(1, 1).start()

    def turn_coarse():
        for t in range(n_c * B // lanes):
            value = vct[:, t * lanes : (t + 1) * lanes].T
            vc[pl.ds(t * (lanes // B), lanes // B)] = value.reshape(lanes // B, B, value.shape[1])

    def turn_fine(start, stop):
        @pl.loop(start // 2, stop // 2)
        def _(pair):
            for slot in range(2):
                i = 2 * pair + slot
                vf_load(i, slot).wait()
                for t in range(v_cols // lanes):
                    value = vft[slot, :, t * lanes : (t + 1) * lanes].T
                    blocks = pl.ds(i * (v_cols // B) + t * (lanes // B), lanes // B)
                    vf[blocks] = value.reshape(lanes // B, B, value.shape[1])

                @pl.when(i + 2 < v_parts)
                def _():
                    vf_load(i + 2, slot).start()

    with jax.named_scope("enter"):
        barrier = pltpu.get_barrier_semaphore()
        for target in (left, right, partner, far):
            pl.semaphore_signal(barrier, inc=1, device_id=target, device_id_type=MESH)
        pl.semaphore_wait(barrier, 4)

    cm_copy = remote(cm, cm_oth, gather_sem.at[0], partner)
    wc_copy = remote(wc_hbm, wc.at[:, pl.ds(half, half), :], gather_sem.at[1], far)
    cb_copy = remote(cb_hbm, cb.at[c], gather_sem.at[2], far)
    up_copy = remote(up_hbm.at[:, :, far_cols], up.at[:, own_rows, :], gather_sem.at[3], far)
    sw_copy = remote(
        sw_hbm.at[:, :, far_cols], sw.at[:, pl.ds(half, half), :], gather_sem.at[4], far
    )
    gathers = [cm_copy, wc_copy, cb_copy, up_copy, sw_copy]
    for copy in gathers:
        copy.start()

    chunk = 8
    steps = n_f // chunk
    rows = chunk * B

    def skip_copy(q):
        part = pl.ds(pl.multiple_of(q * rows, rows), rows)
        return remote(skip.at[part], skip_oth.at[part], skip_sem.at[q], partner)

    with jax.named_scope("wait coarse map"):
        for load in loads[:4]:
            load.wait()
        turn_coarse()
        for copy in (wc_copy, cb_copy, cm_copy):
            copy.wait_recv()
        cm_copy.wait_send()

    @pl.loop(0, steps // 2)
    def _(q):
        skip_copy(q).start()
        skip_copy(steps - 1 - q).start()

    cchunk = 4
    crows = cchunk * B

    def coarse_g(q, k):
        part = pl.ds(pl.multiple_of(q * crows, crows), crows)
        x = jnp.concatenate([cm_own[part, :], cm_oth[part, :]], axis=1)
        return dot(x, wc[k])

    def coarse_first(q):
        blocks = pl.ds(RIM_C + q * cchunk, cchunk)
        ce3[blocks] = coarse_g(q, 3).astype(BF16).reshape(cchunk, B, full)

    def coarse_halo(i, ext):
        sems = halo_c_sem.at[i]
        to_left = remote(
            ext.at[pl.ds(RIM_C, RIM_C)], ext.at[pl.ds(n_c + RIM_C, RIM_C)], sems.at[0], left
        )
        to_right = remote(ext.at[pl.ds(n_c, RIM_C)], ext.at[pl.ds(0, RIM_C)], sems.at[1], right)
        return to_left, to_right

    with jax.named_scope("coarse first"):
        coarse_first(0)
        coarse_first(1)
        coarse_first(n_c // cchunk - 2)
        coarse_first(n_c // cchunk - 1)
        halos = [coarse_halo(0, ce3)]
        for copy in halos[-1]:
            copy.start()

        @pl.loop(2, n_c // cchunk - 2)
        def _(q):
            coarse_first(q)

    with jax.named_scope("coarse g"):
        @pl.loop(0, n_c // cchunk)
        def _(q):
            part = pl.ds(pl.multiple_of(q * cchunk, cchunk), cchunk)
            for k in range(TERMS - 1):
                gc[k, part] = coarse_g(q, k).reshape(cchunk, B, full)

    def coarse_product(ext, r):
        base = p * n_c - RIM_C
        picked = [ext[place_of(jc[j, r] - base, all_c, ext.shape[0])] for j in range(NB)]
        return dot(vc[r], jnp.concatenate(picked, axis=0))

    def coarse_step(q, source, target, k):
        for i in range(cchunk):
            r = q * cchunk + i
            value = gc[k, r] + 2.0 * coarse_product(source, r)
            if k == 1:
                value = value - ce3[RIM_C + r].astype(F32)
            target[RIM_C + r] = value.astype(BF16)

    for i, (source, target, k) in enumerate(((ce3, ce2, 2), (ce2, ce1, 1))):
        turn_fine(2 * i, 2 * i + 2)
        with jax.named_scope(f"coarse halo {k}"):
            for copy in halos[-1]:
                copy.wait_recv()
        for q in (0, 1, n_c // cchunk - 2, n_c // cchunk - 1):
            coarse_step(q, source, target, k)
        halos.append(coarse_halo(i + 1, target))
        for copy in halos[-1]:
            copy.start()

        @pl.loop(2, n_c // cchunk - 2)
        def _(q, source=source, target=target, k=k):
            coarse_step(q, source, target, k)

    turn_fine(4, 6)
    with jax.named_scope("coarse halo 0"):
        for copy in halos[-1]:
            copy.wait_recv()
    with jax.named_scope("coarse last"):
        bias_c = jnp.concatenate([cb[0], cb[1]], axis=1)

        @pl.loop(0, n_c // cchunk)
        def _(q):
            for i in range(cchunk):
                r = q * cchunk + i
                value = gc[0, r] + coarse_product(ce1, r) - ce2[RIM_C + r].astype(F32)
                hidden[r] = jnp.maximum(value + bias_c, 0.0).astype(BF16)

    turn_fine(6, 8)

    for load in loads[4:]:
        load.wait()
    up_copy.wait_recv()
    sw_copy.wait_recv()

    def unpooled(q, k, slot):
        x = hidden[pl.ds(q * cchunk, cchunk)].reshape(crows, full)
        value = dot(x, up[k])
        for i in range(4):
            g[slot, pl.ds(4 * crows * q + i, crows, stride=4), :] = value

    with jax.named_scope("unpool"):
        @pl.loop(0, n_c // cchunk)
        def _(q):
            for k in range(1, TERMS):
                unpooled(q, k, k % 3)

    def fine_part(q):
        return pl.ds(pl.multiple_of(q * rows, rows), rows)

    def joined_g(q, k, slot):
        part = fine_part(q)
        x = jnp.concatenate([skip_own[part, :], skip_oth[part, :]], axis=1)
        return g[slot, part, :] + dot(x, sw[k])

    ends = 2 * RIM_F // chunk

    def put(q, values, own, lo, hi, place):
        blocks = pl.ds(q * chunk, chunk)
        own[blocks] = values
        if place == "lo":
            lo[pl.ds(RIM_F + q * chunk, chunk)] = values
        if place == "hi":
            hi[pl.ds((q - (steps - ends)) * chunk, chunk)] = values

    def fine_halo(i, lo, hi):
        sems = halo_f_sem.at[i]
        to_left = remote(
            lo.at[pl.ds(RIM_F, RIM_F)], hi.at[pl.ds(2 * RIM_F, RIM_F)], sems.at[0], left
        )
        to_right = remote(hi.at[pl.ds(RIM_F, RIM_F)], lo.at[pl.ds(0, RIM_F)], sems.at[1], right)
        return to_left, to_right

    def fine_first(q, place):
        skip_copy(q).wait_recv()
        values = joined_g(q, 3, 0).astype(BF16).reshape(chunk, B, half)
        put(q, values, b3, lo3, hi3, place)

    edge = RIM_F // chunk

    with jax.named_scope("fine first ends"):
        @pl.loop(0, edge)
        def _(q):
            fine_first(q, "lo")

        @pl.loop(steps - edge, steps)
        def _(q):
            fine_first(q, "hi")

    fine_halos = [fine_halo(0, lo3, hi3)]
    for copy in fine_halos[-1]:
        copy.start()

    with jax.named_scope("fine first"):
        @pl.loop(edge, ends)
        def _(q):
            fine_first(q, "lo")

        @pl.loop(steps - ends, steps - edge)
        def _(q):
            fine_first(q, "hi")

        @pl.loop(ends, steps - ends)
        def _(q):
            fine_first(q, None)

    with jax.named_scope("fine g"):
        @pl.loop(0, n_c // cchunk)
        def _(q):
            unpooled(q, 0, 0)

        @pl.loop(0, steps)
        def _(q):
            for k in range(TERMS - 1):
                value = joined_g(q, k, k)
                if k == 0:
                    value = value + fb[...]
                g[k, fine_part(q), :] = value

    def fine_product(source, first, r):
        base = p * n_f + first
        picked = [source[place_of(jf[j, r] - base, all_f, source.shape[0])] for j in range(NB)]
        return dot(vf[r], jnp.concatenate(picked, axis=0))

    def fine_step(q, k, source, first, place):
        for i in range(chunk):
            r = q * chunk + i
            part = pl.ds(pl.multiple_of(r * B, B), B)
            value = fine_product(source, first, r)
            if k == 0:
                value = g[0, part, :] + value - b2[r].astype(F32)
                out[part, :] = value.astype(BF16)
                continue
            value = g[k, part, :] + 2.0 * value
            if k == 1:
                value = value - b3[r].astype(F32)
            value = value.astype(BF16)
            own, lo, hi = ((b1, lo1, hi1), (b2, lo2, hi2))[k - 1]
            own[r] = value
            if place == "lo":
                lo[RIM_F + r] = value
            if place == "hi":
                hi[r - (n_f - 2 * RIM_F)] = value

    def out_copy(q):
        part = fine_part(q)
        return pltpu.make_async_copy(out.at[part], out_hbm.at[part], out_sem.at[q])

    sources = ((b3, lo3, hi3), (b2, lo2, hi2), (b1, lo1, hi1))
    for i, k in enumerate((2, 1, 0)):
        own, lo, hi = sources[i]

        def region(start, stop, source, first, place, k=k):
            @pl.loop(start, stop)
            def _(q):
                fine_step(q, k, source, first, place)
                if k == 0:
                    out_copy(q).start()

        with jax.named_scope(f"fine inner {k}"):
            region(edge, ends, own, 0, "lo")
            region(steps - ends, steps - edge, own, 0, "hi")
            region(ends, steps - ends, own, 0, None)
        with jax.named_scope(f"fine halo {k}"):
            for copy in fine_halos[-1]:
                copy.wait_recv()
        with jax.named_scope(f"fine border {k}"):
            region(0, edge, lo, -RIM_F, "lo")
            region(steps - edge, steps, hi, n_f - 2 * RIM_F, "hi")
        if k > 0:
            fine_halos.append(fine_halo(i + 1, *sources[i + 1][1:]))
            for copy in fine_halos[-1]:
                copy.start()

    with jax.named_scope("finish"):
        @pl.loop(0, steps)
        def _(q):
            skip_copy(q).wait_send()
            out_copy(q).wait()

        for pair in halos + fine_halos:
            for copy in pair:
                copy.wait_send()
        for copy in gathers[1:]:
            copy.wait_send()


def per_device(
    n_patch,
    coarse_map,
    skip_map,
    coarse_values,
    coarse_columns,
    fine_values,
    fine_columns,
    coarse_weight,
    coarse_bias,
    up_weight,
    skip_weight,
    fine_bias,
):
    pixels_c, half = coarse_map.shape
    pixels_f = skip_map.shape[0]
    width = coarse_values.shape[1]
    n_c, n_f = pixels_c // B, pixels_f // B
    full = 2 * half
    steps = n_f // 8
    anywhere = pl.BlockSpec(memory_space=pl.ANY)
    scalars = pl.BlockSpec(memory_space=pltpu.SMEM)
    vmem = pl.BlockSpec(memory_space=pltpu.VMEM)
    dma = pltpu.SemaphoreType.DMA
    border = pltpu.VMEM((3 * RIM_F, B, half), BF16)
    own = pltpu.VMEM((n_f, B, half), BF16)
    coarse_ext = pltpu.VMEM((n_c + 2 * RIM_C, B, full), BF16)
    return pl.pallas_call(
        functools.partial(kernel, n_patch),
        out_shape=jax.ShapeDtypeStruct((pixels_f, half), BF16),
        in_specs=[
            anywhere,
            anywhere,
            anywhere,
            scalars,
            anywhere,
            scalars,
            anywhere,
            anywhere,
            anywhere,
            anywhere,
            vmem,
        ],
        out_specs=anywhere,
        scratch_shapes=[
            pltpu.VMEM((pixels_c, half), BF16),
            pltpu.VMEM((pixels_c, half), BF16),
            pltpu.VMEM((n_c, B, width), BF16),
            pltpu.VMEM((TERMS, full, full), BF16),
            pltpu.VMEM((2, 1, half), F32),
            pltpu.VMEM((TERMS, full, half), BF16),
            pltpu.VMEM((TERMS, full, half), BF16),
            pltpu.VMEM((pixels_f, half), BF16),
            pltpu.VMEM((pixels_f, half), BF16),
            pltpu.VMEM((n_f, B, width), BF16),
            coarse_ext,
            coarse_ext,
            coarse_ext,
            pltpu.VMEM((TERMS - 1, n_c, B, full), F32),
            pltpu.VMEM((n_c, B, full), BF16),
            pltpu.VMEM((TERMS - 1, pixels_f, half), F32),
            own,
            own,
            own,
            border,
            border,
            border,
            border,
            border,
            border,
            pltpu.VMEM((pixels_f, half), BF16),
            pltpu.VMEM((width, pixels_c), BF16),
            pltpu.VMEM((2, width, 1024), BF16),
            dma((7,)),
            dma((2,)),
            dma((5, 2)),
            dma((steps, 2)),
            dma((3, 2, 2)),
            dma((3, 2, 2)),
            dma((steps,)),
        ],
        compiler_params=pltpu.CompilerParams(
            collective_id=0, has_side_effects=True, vmem_limit_bytes=63 * 1024 * 1024
        ),
    )(
        coarse_map,
        skip_map,
        coarse_values.T,
        coarse_columns.T,
        fine_values.T,
        fine_columns.T,
        coarse_weight,
        coarse_bias.reshape(1, half),
        up_weight,
        skip_weight,
        fine_bias.reshape(1, half),
    )


def solution(mesh):
    placed = (
        P("patch", "chan"),
        P("patch", "chan"),
        P("patch", None),
        P("patch", None),
        P("patch", None),
        P("patch", None),
        P(None, "chan", None),
        P("chan"),
        P(None, "chan", None),
        P(None, "chan", None),
        P("chan"),
    )
    return jax.shard_map(
        functools.partial(per_device, mesh.shape["patch"]),
        mesh=mesh,
        in_specs=placed,
        out_specs=P("patch", "chan"),
        check_vma=False,
    )
```

```python
import functools

import jax
import jax.numpy as jnp
from jax import lax
from jax.experimental import pallas as pl
from jax.experimental.pallas import tpu as pltpu
from jax.sharding import PartitionSpec as P

B = 64
NB = 9
RIM_C = 8
RIM_F = 16
TERMS = 4
FLIP = 8
F32 = jnp.float32
BF16 = jnp.bfloat16
MESH = pl.DeviceIdType.MESH


def dot(a, b):
    return jnp.dot(a, b, preferred_element_type=F32)


def place_of(offset, blocks_all, held):
    return jnp.minimum(lax.bitwise_and(offset, blocks_all - 1), held - 1)


def kernel(
    n_patch,
    cm,
    skip,
    vc_hbm,
    jc,
    vf_hbm,
    jf,
    wc_hbm,
    cb_hbm,
    up_hbm,
    sw_hbm,
    fb,
    out,
    cm_own,
    cm_oth,
    vc,
    wc,
    cb,
    up,
    sw,
    skip_own,
    skip_oth,
    vf,
    turned,
    coarse_own,
    coarse_lo,
    coarse_hi,
    gc,
    hidden,
    g,
    fine_own,
    fine_lo,
    fine_hi,
    load_sem,
    turn_sem,
    gather_sem,
    skip_sem,
    halo_c_sem,
    halo_f_sem,
):
    p = lax.axis_index("patch")
    c = lax.axis_index("chan")
    left = (lax.rem(p + n_patch - 1, n_patch), c)
    right = (lax.rem(p + 1, n_patch), c)
    partner = (p, 1 - c)
    z_hi = lax.rem(p // FLIP, 2)
    far = (p + FLIP - 2 * FLIP * z_hi, 1 - c)

    n_c = vc.shape[0]
    n_f = vf.shape[0]
    all_c = n_c * n_patch
    all_f = n_f * n_patch
    half = cm.shape[1]
    full = 2 * half

    def remote(src, dst, sems, target):
        return pltpu.make_async_remote_copy(
            src_ref=src,
            dst_ref=dst,
            send_sem=sems.at[0],
            recv_sem=sems.at[1],
            device_id=target,
            device_id_type=MESH,
        )

    own_rows = pl.ds(pl.multiple_of(c * half, half), half)
    own_cols = own_rows
    far_cols = pl.ds(pl.multiple_of((1 - c) * half, half), half)

    lanes = 128
    cols = turned.shape[2]
    c_parts = n_c * B // cols
    f_parts = n_f * B // cols

    def entries(source, i, slot):
        part = pl.ds(pl.multiple_of(i * cols, cols), cols)
        return pltpu.make_async_copy(source.at[:, part], turned.at[slot], turn_sem.at[slot])

    def turn(target, i, slot):
        for t in range(cols // lanes):
            value = turned[slot, :, t * lanes : (t + 1) * lanes].T
            blocks = pl.ds(i * (cols // B) + t * (lanes // B), lanes // B)
            target[blocks] = value.reshape(lanes // B, B, value.shape[1])

    def turn_coarse():
        for i in range(c_parts):
            slot = i % 2
            entries(vc_hbm, i, slot).wait()
            turn(vc, i, slot)
            if i + 2 < c_parts:
                entries(vc_hbm, i + 2, slot).start()
            else:
                entries(vf_hbm, i + 2 - c_parts, slot).start()

    def turn_fine(start, stop):
        @pl.loop(start // 2, stop // 2)
        def _(pair):
            for slot in range(2):
                i = 2 * pair + slot
                entries(vf_hbm, i, slot).wait()
                turn(vf, i, slot)

                @pl.when(i + 2 < f_parts)
                def _():
                    entries(vf_hbm, i + 2, slot).start()

    pairs = [
        (cm, cm_own),
        (wc_hbm, wc.at[:, pl.ds(0, half), :]),
        (cb_hbm, cb.at[c]),
        (up_hbm.at[:, :, own_cols], up.at[:, own_rows, :]),
        (sw_hbm.at[:, :, own_cols], sw.at[:, pl.ds(0, half), :]),
        (skip, skip_own),
    ]
    loads = [pltpu.make_async_copy(a, b, load_sem.at[i]) for i, (a, b) in enumerate(pairs)]
    entries(vc_hbm, 0, 0).start()
    entries(vc_hbm, 1, 1).start()
    for load in loads:
        load.start()

    barrier = pltpu.get_barrier_semaphore()
    for target in (left, right, partner, far):
        pl.semaphore_signal(barrier, inc=1, device_id=target, device_id_type=MESH)
    pl.semaphore_wait(barrier, 4)

    cm_copy = remote(cm, cm_oth, gather_sem.at[0], partner)
    wc_copy = remote(wc_hbm, wc.at[:, pl.ds(half, half), :], gather_sem.at[1], far)
    cb_copy = remote(cb_hbm, cb.at[c], gather_sem.at[2], far)
    up_copy = remote(up_hbm.at[:, :, far_cols], up.at[:, own_rows, :], gather_sem.at[3], far)
    sw_copy = remote(
        sw_hbm.at[:, :, far_cols], sw.at[:, pl.ds(half, half), :], gather_sem.at[4], far
    )
    gathers = [cm_copy, wc_copy, cb_copy, up_copy, sw_copy]
    for copy in gathers:
        copy.start()

    chunk = 8
    steps = n_f // chunk
    rows = chunk * B

    def skip_copy(q):
        part = pl.ds(pl.multiple_of(q * rows, rows), rows)
        return remote(skip.at[part], skip_oth.at[part], skip_sem.at[q], partner)

    for load in loads[:3]:
        load.wait()
    turn_coarse()
    for copy in (wc_copy, cb_copy, cm_copy):
        copy.wait_recv()
    cm_copy.wait_send()

    def skip_send(*pair_numbers):
        for q in pair_numbers:
            skip_copy(q).start()
            skip_copy(steps - 1 - q).start()

    skip_send(0, 1)

    def coarse_keep(slot, r, values):
        coarse_own[slot][r] = values
        if r < n_c // 2:
            coarse_lo[slot][RIM_C + r] = values
        else:
            coarse_hi[slot][r - n_c // 2] = values

    def coarse_g(first, count, k):
        part = pl.ds(first * B, count * B)
        x = jnp.concatenate([cm_own[part, :], cm_oth[part, :]], axis=1)
        return dot(x, wc[k])

    def coarse_halo(slot):
        sems = halo_c_sem.at[slot]
        to_left = remote(
            coarse_lo[slot].at[pl.ds(RIM_C, RIM_C)],
            coarse_hi[slot].at[pl.ds(n_c // 2, RIM_C)],
            sems.at[0],
            left,
        )
        to_right = remote(
            coarse_hi[slot].at[pl.ds(n_c // 2 - RIM_C, RIM_C)],
            coarse_lo[slot].at[pl.ds(0, RIM_C)],
            sems.at[1],
            right,
        )
        return to_left, to_right

    def coarse_first(first):
        values = coarse_g(first, RIM_C, 3).astype(BF16).reshape(RIM_C, B, full)
        for i in range(RIM_C):
            coarse_keep(0, first + i, values[i])

    coarse_first(0)
    coarse_first(n_c - RIM_C)
    halos = [coarse_halo(0)]
    for copy in halos[-1]:
        copy.start()
    for first in range(RIM_C, n_c - RIM_C, RIM_C):
        coarse_first(first)

    @pl.loop(0, n_c // RIM_C)
    def _(q):
        part = pl.ds(pl.multiple_of(q * RIM_C * B, RIM_C * B), RIM_C * B)
        x = jnp.concatenate([cm_own[part, :], cm_oth[part, :]], axis=1)
        for k in range(TERMS - 1):
            value = dot(x, wc[k])
            gc[2 * k, part, :] = value[:, :half]
            gc[2 * k + 1, part, :] = value[:, half:]

    skip_send(2)
    bias_c = jnp.concatenate([cb[0], cb[1]], axis=1)

    def coarse_rows(slot, numbers):
        k = 2 - slot
        for r in numbers:
            if r < RIM_C:
                source, first = coarse_lo, -RIM_C
            elif r >= n_c - RIM_C:
                source, first = coarse_hi, n_c // 2
            else:
                source, first = coarse_own, 0
            base = p * n_c + first
            picked = [
                source[slot][place_of(jc[j, r] - base, all_c, source[slot].shape[0])] for j in range(NB)
            ]
            value = dot(vc[r], jnp.concatenate(picked, axis=0))
            part = pl.ds(r * B, B)
            term = jnp.concatenate([gc[2 * k, part, :], gc[2 * k + 1, part, :]], axis=1)
            if k > 0:
                value = 2.0 * value
            value = term + value
            if slot > 0:
                value = value - coarse_own[slot - 1][r].astype(F32)
            if k > 0:
                coarse_keep(slot + 1, r, value.astype(BF16))
            else:
                hidden[r] = jnp.maximum(value + bias_c, 0.0).astype(BF16)

    for slot in range(3):
        coarse_rows(slot, range(RIM_C, n_c - RIM_C))
        skip_send(3 + slot)
        turn_fine(slot * (f_parts // 4), (slot + 1) * (f_parts // 4))
        for copy in halos[-1]:
            copy.wait_recv()
        coarse_rows(slot, [*range(RIM_C), *range(n_c - RIM_C, n_c)])
        if slot < 2:
            halos.append(coarse_halo(slot + 1))
            for copy in halos[-1]:
                copy.start()

    for load in loads[3:]:
        load.wait()
    up_copy.wait_recv()
    sw_copy.wait_recv()
    quarter = gc.shape[1]

    @pl.loop(0, n_c // 4)
    def _(q):
        count = 4 * B
        x = hidden[pl.ds(q * 4, 4)].reshape(count, full)
        low = dot(x, jnp.concatenate([up[0], up[1]], axis=1))
        high = dot(x, jnp.concatenate([up[2], up[3]], axis=1))
        slot = 2 + (4 * count * q) // quarter
        start = (4 * count * q) % quarter
        for i in range(4):
            part = pl.ds(4 * count * q + i, count, stride=4)
            g[0, part, :] = low[:, :half] + fb[...]
            g[1, part, :] = low[:, half:]
            g[2, part, :] = high[:, :half]
            gc[slot, pl.ds(start + i, count, stride=4), :] = high[:, half:]

    skip_send(6)
    turn_fine(3 * (f_parts // 4), f_parts)
    skip_send(7)

    edge = RIM_F // chunk
    ends = 2 * edge

    def fine_keep(slot, near, i, r, values):
        fine_own[slot][r] = values
        if near == "lo":
            fine_lo[slot][RIM_F + r] = values
        if near == "hi":
            fine_hi[slot][r - (n_f - 2 * RIM_F)] = values

    def both(q, near):
        return ((q, "lo" if near else None), (steps - 1 - q, "hi" if near else None))

    def fine_first(q, near):
        for at, side in both(q, near):
            skip_copy(at).wait_recv()
        for at, side in both(q, near):
            part = pl.ds(pl.multiple_of(at * rows, rows), rows)
            x = jnp.concatenate([skip_own[part, :], skip_oth[part, :]], axis=1)
            low = dot(x, jnp.concatenate([sw[0], sw[1]], axis=1))
            high = dot(x, jnp.concatenate([sw[2], sw[3]], axis=1))
            g[0, part, :] += low[:, :half]
            g[1, part, :] += low[:, half:]
            g[2, part, :] += high[:, :half]
            slot = 2 + (at * rows) // quarter
            start = pl.multiple_of((at * rows) % quarter, rows)
            value = high[:, half:] + gc[slot, pl.ds(start, rows), :]
            value = value.astype(BF16).reshape(chunk, B, half)
            for i in range(chunk):
                fine_keep(0, side, i, at * chunk + i, value[i])

    def fine_halo(slot):
        sems = halo_f_sem.at[slot]
        to_left = remote(
            fine_lo[slot].at[pl.ds(RIM_F, RIM_F)],
            fine_hi[slot].at[pl.ds(2 * RIM_F, RIM_F)],
            sems.at[0],
            left,
        )
        to_right = remote(
            fine_hi[slot].at[pl.ds(RIM_F, RIM_F)],
            fine_lo[slot].at[pl.ds(0, RIM_F)],
            sems.at[1],
            right,
        )
        return to_left, to_right

    def fine_rows(slot, q, near, border=False):
        k = 2 - slot
        for at, side in both(q, near):
            if not border:
                source, first = fine_own, 0
            elif side == "lo":
                source, first = fine_lo, -RIM_F
            else:
                source, first = fine_hi, n_f - 2 * RIM_F
            base = p * n_f + first
            for i in range(chunk):
                r = at * chunk + i
                part = pl.ds(pl.multiple_of(r * B, B), B)
                picked = [
                    source[slot][place_of(jf[j, r] - base, all_f, source[slot].shape[0])]
                    for j in range(NB)
                ]
                value = dot(vf[r], jnp.concatenate(picked, axis=0))
                if k > 0:
                    value = 2.0 * value
                value = g[k, part, :] + value
                if slot > 0:
                    value = value - fine_own[slot - 1][r].astype(F32)
                value = value.astype(BF16)
                if k > 0:
                    fine_keep(slot + 1, side, i, r, value)
                else:
                    out[part, :] = value

    fine_halos = []

    def send(slot):
        fine_halos.append(fine_halo(slot))
        for copy in fine_halos[-1]:
            copy.start()

    def arrived(slot):
        for copy in fine_halos[slot]:
            copy.wait_recv()

    def run(start, stop, body):
        if stop - start == 1:
            body(start)
        else:
            pl.loop(start, stop)(body)

    def first_of(start, stop, near):
        run(start, stop, lambda q: fine_first(q, near))

    def rows_of(slot, start, stop, near, border=False):
        run(start, stop, lambda q: fine_rows(slot, q, near, border))

    middle = steps // 2
    first_of(0, edge, True)
    send(0)
    first_of(edge, ends, True)
    first_of(ends, ends + 2, False)
    rows_of(0, edge, ends, True)
    arrived(0)
    rows_of(0, 0, edge, True, True)
    send(1)
    first_of(ends + 2, ends + 3, False)
    rows_of(0, ends, ends + 1, False)
    first_of(ends + 3, middle, False)
    rows_of(0, ends + 1, middle, False)
    rows_of(1, ends, middle, False)
    arrived(1)
    rows_of(1, 0, edge, True, True)
    send(2)
    rows_of(1, edge, ends, True)
    rows_of(2, edge, middle, False)
    arrived(2)
    rows_of(2, 0, edge, True, True)

    @pl.loop(0, steps)
    def _(q):
        skip_copy(q).wait_send()

    for pair in halos + fine_halos:
        for copy in pair:
            copy.wait_send()
    for copy in gathers[1:]:
        copy.wait_send()


def per_device(
    n_patch,
    coarse_map,
    skip_map,
    coarse_values,
    coarse_columns,
    fine_values,
    fine_columns,
    coarse_weight,
    coarse_bias,
    up_weight,
    skip_weight,
    fine_bias,
):
    pixels_c, half = coarse_map.shape
    pixels_f = skip_map.shape[0]
    width = coarse_values.shape[1]
    n_c, n_f = pixels_c // B, pixels_f // B
    full = 2 * half
    steps = n_f // 8
    anywhere = pl.BlockSpec(memory_space=pl.ANY)
    scalars = pl.BlockSpec(memory_space=pltpu.SMEM)
    vmem = pl.BlockSpec(memory_space=pltpu.VMEM)
    dma = pltpu.SemaphoreType.DMA
    return pl.pallas_call(
        functools.partial(kernel, n_patch),
        out_shape=pltpu.VMEM((pixels_f, half), BF16),
        in_specs=[
            anywhere,
            anywhere,
            anywhere,
            scalars,
            anywhere,
            scalars,
            anywhere,
            anywhere,
            anywhere,
            anywhere,
            vmem,
        ],
        out_specs=vmem,
        scratch_shapes=[
            pltpu.VMEM((pixels_c, half), BF16),
            pltpu.VMEM((pixels_c, half), BF16),
            pltpu.VMEM((n_c, B, width), BF16),
            pltpu.VMEM((TERMS, full, full), BF16),
            pltpu.VMEM((2, 1, half), F32),
            pltpu.VMEM((TERMS, full, half), BF16),
            pltpu.VMEM((TERMS, full, half), BF16),
            pltpu.VMEM((pixels_f, half), BF16),
            pltpu.VMEM((pixels_f, half), BF16),
            pltpu.VMEM((n_f, B, width), BF16),
            pltpu.VMEM((2, width, 512), BF16),
            [pltpu.VMEM((n_c, B, full), BF16)] * 3,
            [pltpu.VMEM((n_c // 2 + RIM_C, B, full), BF16)] * 3,
            [pltpu.VMEM((n_c // 2 + RIM_C, B, full), BF16)] * 3,
            pltpu.VMEM((2 * (TERMS - 1), pixels_c, half), F32),
            pltpu.VMEM((n_c, B, full), BF16),
            pltpu.VMEM((TERMS - 1, pixels_f, half), F32),
            [pltpu.VMEM((n_f, B, half), BF16)] * 3,
            [pltpu.VMEM((3 * RIM_F, B, half), BF16)] * 3,
            [pltpu.VMEM((3 * RIM_F, B, half), BF16)] * 3,
            dma((6,)),
            dma((2,)),
            dma((5, 2)),
            dma((steps, 2)),
            dma((3, 2, 2)),
            dma((3, 2, 2)),
        ],
        compiler_params=pltpu.CompilerParams(
            collective_id=0, has_side_effects=True, vmem_limit_bytes=60 * 1024 * 1024
        ),
    )(
        coarse_map,
        skip_map,
        coarse_values.T,
        coarse_columns.T,
        fine_values.T,
        fine_columns.T,
        coarse_weight,
        coarse_bias.reshape(1, half),
        up_weight,
        skip_weight,
        fine_bias.reshape(1, half),
    )


def solution(mesh):
    placed = (
        P("patch", "chan"),
        P("patch", "chan"),
        P("patch", None),
        P("patch", None),
        P("patch", None),
        P("patch", None),
        P(None, "chan", None),
        P("chan"),
        P(None, "chan", None),
        P(None, "chan", None),
        P("chan"),
    )
    return jax.shard_map(
        functools.partial(per_device, mesh.shape["patch"]),
        mesh=mesh,
        in_specs=placed,
        out_specs=P("patch", "chan"),
        check_vma=False,
    )
```

```python
import functools

import jax
import jax.numpy as jnp
from jax import lax
from jax.experimental import pallas as pl
from jax.experimental.pallas import tpu as pltpu
from jax.sharding import PartitionSpec as P

B = 64
NB = 9
RIM_C = 8
RIM_F = 16
TERMS = 4
FLIP = 8
F32 = jnp.float32
BF16 = jnp.bfloat16
MESH = pl.DeviceIdType.MESH


def dot(a, b):
    return jnp.dot(a, b, preferred_element_type=F32)


def place_of(offset, blocks_all, held):
    return jnp.minimum(lax.bitwise_and(offset, blocks_all - 1), held - 1)


def kernel(
    n_patch,
    cm,
    skip,
    vc_hbm,
    jc,
    vf_hbm,
    jf,
    wc_hbm,
    cb_hbm,
    up_hbm,
    sw_hbm,
    fb,
    out,
    cm_own,
    cm_oth,
    vc,
    wc,
    cb,
    up,
    sw,
    skip_own,
    skip_oth,
    vf,
    turned,
    coarse_own,
    coarse_lo,
    coarse_hi,
    gc,
    hidden,
    g,
    fine_own,
    fine_lo,
    fine_hi,
    load_sem,
    turn_sem,
    gather_sem,
    skip_sem,
    halo_c_sem,
    halo_f_sem,
):
    p = lax.axis_index("patch")
    c = lax.axis_index("chan")
    left = (lax.rem(p + n_patch - 1, n_patch), c)
    right = (lax.rem(p + 1, n_patch), c)
    partner = (p, 1 - c)
    row = lax.rem(p, FLIP)
    coarse_left = (left[0], jnp.where(row == 0, 1 - c, c))
    coarse_right = (right[0], jnp.where(row == FLIP - 1, 1 - c, c))
    z_hi = lax.rem(p // FLIP, 2)
    far = (p + FLIP - 2 * FLIP * z_hi, 1 - c)

    n_c = vc.shape[0]
    n_f = vf.shape[0]
    all_c = n_c * n_patch
    all_f = n_f * n_patch
    half = cm.shape[1]
    full = 2 * half

    def remote(src, dst, sems, target):
        return pltpu.make_async_remote_copy(
            src_ref=src,
            dst_ref=dst,
            send_sem=sems.at[0],
            recv_sem=sems.at[1],
            device_id=target,
            device_id_type=MESH,
        )

    own_rows = pl.ds(pl.multiple_of(c * half, half), half)
    own_cols = own_rows
    far_cols = pl.ds(pl.multiple_of((1 - c) * half, half), half)

    lanes = 128
    cols = turned.shape[2]
    c_parts = n_c * B // cols
    f_parts = n_f * B // cols

    def entries(source, i, slot):
        part = pl.ds(pl.multiple_of(i * cols, cols), cols)
        return pltpu.make_async_copy(source.at[:, part], turned.at[slot], turn_sem.at[slot])

    def turn(target, i, slot):
        for t in range(cols // lanes):
            value = turned[slot, :, t * lanes : (t + 1) * lanes].T
            blocks = pl.ds(i * (cols // B) + t * (lanes // B), lanes // B)
            target[blocks] = value.reshape(lanes // B, B, value.shape[1])

    def turn_coarse():
        for i in range(c_parts):
            slot = i % 2
            entries(vc_hbm, i, slot).wait()
            turn(vc, i, slot)
            if i + 2 < c_parts:
                entries(vc_hbm, i + 2, slot).start()
            else:
                entries(vf_hbm, i + 2 - c_parts, slot).start()

    def turn_fine(start, stop):
        @pl.loop(start // 2, stop // 2)
        def _(pair):
            for slot in range(2):
                i = 2 * pair + slot
                entries(vf_hbm, i, slot).wait()
                turn(vf, i, slot)

                @pl.when(i + 2 < f_parts)
                def _():
                    entries(vf_hbm, i + 2, slot).start()

    pairs = [
        (cm, cm_own),
        (wc_hbm, wc.at[:, pl.ds(0, half), :]),
        (cb_hbm, cb.at[c]),
        (up_hbm.at[:, :, own_cols], up.at[:, own_rows, :]),
        (sw_hbm.at[:, :, own_cols], sw.at[:, pl.ds(0, half), :]),
        (skip, skip_own),
    ]
    loads = [pltpu.make_async_copy(a, b, load_sem.at[i]) for i, (a, b) in enumerate(pairs)]
    entries(vc_hbm, 0, 0).start()
    entries(vc_hbm, 1, 1).start()
    for load in loads:
        load.start()

    barrier = pltpu.get_barrier_semaphore()
    for target in (left, right, coarse_left, coarse_right, partner, far):
        pl.semaphore_signal(barrier, inc=1, device_id=target, device_id_type=MESH)
    pl.semaphore_wait(barrier, 6)

    cm_copy = remote(cm, cm_oth, gather_sem.at[0], partner)
    wc_copy = remote(wc_hbm, wc.at[:, pl.ds(half, half), :], gather_sem.at[1], far)
    cb_copy = remote(cb_hbm, cb.at[c], gather_sem.at[2], far)
    up_copy = remote(up_hbm.at[:, :, far_cols], up.at[:, own_rows, :], gather_sem.at[3], far)
    sw_copy = remote(
        sw_hbm.at[:, :, far_cols], sw.at[:, pl.ds(half, half), :], gather_sem.at[4], far
    )
    gathers = [cm_copy, wc_copy, cb_copy, up_copy, sw_copy]
    for copy in gathers:
        copy.start()

    chunk = 8
    steps = n_f // chunk
    rows = chunk * B

    def skip_copy(q):
        part = pl.ds(pl.multiple_of(q * rows, rows), rows)
        return remote(skip.at[part], skip_oth.at[part], skip_sem.at[q], partner)

    for load in loads[:3]:
        load.wait()
    turn_coarse()
    for copy in (wc_copy, cb_copy, cm_copy):
        copy.wait_recv()
    cm_copy.wait_send()

    def skip_send(*pair_numbers):
        for q in pair_numbers:
            skip_copy(q).start()
            skip_copy(steps - 1 - q).start()

    skip_send(0, 1)

    def coarse_keep(slot, r, values):
        coarse_own[slot][r] = values
        if r < n_c // 2:
            coarse_lo[slot][RIM_C + r] = values
        else:
            coarse_hi[slot][r - n_c // 2] = values

    def coarse_g(first, count, k):
        part = pl.ds(first * B, count * B)
        x = jnp.concatenate([cm_own[part, :], cm_oth[part, :]], axis=1)
        return dot(x, wc[k])

    def coarse_halo(slot):
        sems = halo_c_sem.at[slot]
        to_left = remote(
            coarse_lo[slot].at[pl.ds(RIM_C, RIM_C)],
            coarse_hi[slot].at[pl.ds(n_c // 2, RIM_C)],
            sems.at[0],
            coarse_left,
        )
        to_right = remote(
            coarse_hi[slot].at[pl.ds(n_c // 2 - RIM_C, RIM_C)],
            coarse_lo[slot].at[pl.ds(0, RIM_C)],
            sems.at[1],
            coarse_right,
        )
        return to_left, to_right

    def coarse_first(first):
        values = coarse_g(first, RIM_C, 3).astype(BF16).reshape(RIM_C, B, full)
        for i in range(RIM_C):
            coarse_keep(0, first + i, values[i])

    coarse_first(0)
    coarse_first(n_c - RIM_C)
    halos = [coarse_halo(0)]
    for copy in halos[-1]:
        copy.start()
    for first in range(RIM_C, n_c - RIM_C, RIM_C):
        coarse_first(first)

    @pl.loop(0, n_c // RIM_C)
    def _(q):
        part = pl.ds(pl.multiple_of(q * RIM_C * B, RIM_C * B), RIM_C * B)
        x = jnp.concatenate([cm_own[part, :], cm_oth[part, :]], axis=1)
        for k in range(TERMS - 1):
            value = dot(x, wc[k])
            gc[2 * k, part, :] = value[:, :half]
            gc[2 * k + 1, part, :] = value[:, half:]

    skip_send(2)
    bias_c = jnp.concatenate([cb[0], cb[1]], axis=1)

    def coarse_rows(slot, numbers):
        k = 2 - slot
        for r in numbers:
            if r < RIM_C:
                source, first = coarse_lo, -RIM_C
            elif r >= n_c - RIM_C:
                source, first = coarse_hi, n_c // 2
            else:
                source, first = coarse_own, 0
            base = p * n_c + first
            picked = [
                source[slot][place_of(jc[j, r] - base, all_c, source[slot].shape[0])] for j in range(NB)
            ]
            value = dot(vc[r], jnp.concatenate(picked, axis=0))
            part = pl.ds(r * B, B)
            term = jnp.concatenate([gc[2 * k, part, :], gc[2 * k + 1, part, :]], axis=1)
            if k > 0:
                value = 2.0 * value
            value = term + value
            if slot > 0:
                value = value - coarse_own[slot - 1][r].astype(F32)
            if k > 0:
                coarse_keep(slot + 1, r, value.astype(BF16))
            else:
                hidden[r] = jnp.maximum(value + bias_c, 0.0).astype(BF16)

    for slot in range(3):
        coarse_rows(slot, range(RIM_C, n_c - RIM_C))
        skip_send(3 + slot)
        turn_fine(slot * (f_parts // 4), (slot + 1) * (f_parts // 4))
        for copy in halos[-1]:
            copy.wait_recv()
        coarse_rows(slot, [*range(RIM_C), *range(n_c - RIM_C, n_c)])
        if slot < 2:
            halos.append(coarse_halo(slot + 1))
            for copy in halos[-1]:
                copy.start()

    for load in loads[3:]:
        load.wait()
    up_copy.wait_recv()
    sw_copy.wait_recv()
    quarter = gc.shape[1]

    @pl.loop(0, n_c // 4)
    def _(q):
        count = 4 * B
        x = hidden[pl.ds(q * 4, 4)].reshape(count, full)
        low = dot(x, jnp.concatenate([up[0], up[1]], axis=1))
        high = dot(x, jnp.concatenate([up[2], up[3]], axis=1))
        slot = 2 + (4 * count * q) // quarter
        start = (4 * count * q) % quarter
        for i in range(4):
            part = pl.ds(4 * count * q + i, count, stride=4)
            g[0, part, :] = low[:, :half] + fb[...]
            g[1, part, :] = low[:, half:]
            g[2, part, :] = high[:, :half]
            gc[slot, pl.ds(start + i, count, stride=4), :] = high[:, half:]

    skip_send(6)
    turn_fine(3 * (f_parts // 4), f_parts)
    skip_send(7)

    edge = RIM_F // chunk
    ends = 2 * edge

    def fine_keep(slot, near, i, r, values):
        fine_own[slot][r] = values
        if near == "lo":
            fine_lo[slot][RIM_F + r] = values
        if near == "hi":
            fine_hi[slot][r - (n_f - 2 * RIM_F)] = values

    def both(q, near):
        return ((q, "lo" if near else None), (steps - 1 - q, "hi" if near else None))

    def fine_first(q, near):
        for at, side in both(q, near):
            skip_copy(at).wait_recv()
        for at, side in both(q, near):
            part = pl.ds(pl.multiple_of(at * rows, rows), rows)
            x = jnp.concatenate([skip_own[part, :], skip_oth[part, :]], axis=1)
            low = dot(x, jnp.concatenate([sw[0], sw[1]], axis=1))
            high = dot(x, jnp.concatenate([sw[2], sw[3]], axis=1))
            g[0, part, :] += low[:, :half]
            g[1, part, :] += low[:, half:]
            g[2, part, :] += high[:, :half]
            slot = 2 + (at * rows) // quarter
            start = pl.multiple_of((at * rows) % quarter, rows)
            value = high[:, half:] + gc[slot, pl.ds(start, rows), :]
            value = value.astype(BF16).reshape(chunk, B, half)
            for i in range(chunk):
                fine_keep(0, side, i, at * chunk + i, value[i])

    def fine_halo(slot):
        sems = halo_f_sem.at[slot]
        to_left = remote(
            fine_lo[slot].at[pl.ds(RIM_F, RIM_F)],
            fine_hi[slot].at[pl.ds(2 * RIM_F, RIM_F)],
            sems.at[0],
            left,
        )
        to_right = remote(
            fine_hi[slot].at[pl.ds(RIM_F, RIM_F)],
            fine_lo[slot].at[pl.ds(0, RIM_F)],
            sems.at[1],
            right,
        )
        return to_left, to_right

    def fine_rows(slot, q, near, border=False):
        k = 2 - slot
        for at, side in both(q, near):
            if not border:
                source, first = fine_own, 0
            elif side == "lo":
                source, first = fine_lo, -RIM_F
            else:
                source, first = fine_hi, n_f - 2 * RIM_F
            base = p * n_f + first
            for i in range(chunk):
                r = at * chunk + i
                part = pl.ds(pl.multiple_of(r * B, B), B)
                picked = [
                    source[slot][place_of(jf[j, r] - base, all_f, source[slot].shape[0])]
                    for j in range(NB)
                ]
                value = dot(vf[r], jnp.concatenate(picked, axis=0))
                if k > 0:
                    value = 2.0 * value
                value = g[k, part, :] + value
                if slot > 0:
                    value = value - fine_own[slot - 1][r].astype(F32)
                value = value.astype(BF16)
                if k > 0:
                    fine_keep(slot + 1, side, i, r, value)
                else:
                    out[part, :] = value

    fine_halos = []

    def send(slot):
        fine_halos.append(fine_halo(slot))
        for copy in fine_halos[-1]:
            copy.start()

    def arrived(slot):
        for copy in fine_halos[slot]:
            copy.wait_recv()

    def run(start, stop, body):
        if stop - start == 1:
            body(start)
        else:
            pl.loop(start, stop)(body)

    def first_of(start, stop, near):
        run(start, stop, lambda q: fine_first(q, near))

    def rows_of(slot, start, stop, near, border=False):
        run(start, stop, lambda q: fine_rows(slot, q, near, border))

    middle = steps // 2
    first_of(0, edge, True)
    send(0)
    first_of(edge, ends, True)
    first_of(ends, ends + 2, False)
    rows_of(0, edge, ends, True)
    arrived(0)
    rows_of(0, 0, edge, True, True)
    send(1)
    first_of(ends + 2, ends + 3, False)
    rows_of(0, ends, ends + 1, False)
    first_of(ends + 3, middle, False)
    rows_of(0, ends + 1, middle, False)
    rows_of(1, ends, middle, False)
    arrived(1)
    rows_of(1, 0, edge, True, True)
    send(2)
    rows_of(1, edge, ends, True)
    rows_of(2, edge, middle, False)
    arrived(2)
    rows_of(2, 0, edge, True, True)

    @pl.loop(0, steps)
    def _(q):
        skip_copy(q).wait_send()

    for pair in halos + fine_halos:
        for copy in pair:
            copy.wait_send()
    for copy in gathers[1:]:
        copy.wait_send()


def per_device(
    n_patch,
    coarse_map,
    skip_map,
    coarse_values,
    coarse_columns,
    fine_values,
    fine_columns,
    coarse_weight,
    coarse_bias,
    up_weight,
    skip_weight,
    fine_bias,
):
    pixels_c, half = coarse_map.shape
    pixels_f = skip_map.shape[0]
    width = coarse_values.shape[1]
    n_c, n_f = pixels_c // B, pixels_f // B
    full = 2 * half
    steps = n_f // 8
    anywhere = pl.BlockSpec(memory_space=pl.ANY)
    scalars = pl.BlockSpec(memory_space=pltpu.SMEM)
    vmem = pl.BlockSpec(memory_space=pltpu.VMEM)
    dma = pltpu.SemaphoreType.DMA
    return pl.pallas_call(
        functools.partial(kernel, n_patch),
        out_shape=pltpu.VMEM((pixels_f, half), BF16),
        in_specs=[
            anywhere,
            anywhere,
            anywhere,
            scalars,
            anywhere,
            scalars,
            anywhere,
            anywhere,
            anywhere,
            anywhere,
            vmem,
        ],
        out_specs=vmem,
        scratch_shapes=[
            pltpu.VMEM((pixels_c, half), BF16),
            pltpu.VMEM((pixels_c, half), BF16),
            pltpu.VMEM((n_c, B, width), BF16),
            pltpu.VMEM((TERMS, full, full), BF16),
            pltpu.VMEM((2, 1, half), F32),
            pltpu.VMEM((TERMS, full, half), BF16),
            pltpu.VMEM((TERMS, full, half), BF16),
            pltpu.VMEM((pixels_f, half), BF16),
            pltpu.VMEM((pixels_f, half), BF16),
            pltpu.VMEM((n_f, B, width), BF16),
            pltpu.VMEM((2, width, 512), BF16),
            [pltpu.VMEM((n_c, B, full), BF16)] * 3,
            [pltpu.VMEM((n_c // 2 + RIM_C, B, full), BF16)] * 3,
            [pltpu.VMEM((n_c // 2 + RIM_C, B, full), BF16)] * 3,
            pltpu.VMEM((2 * (TERMS - 1), pixels_c, half), F32),
            pltpu.VMEM((n_c, B, full), BF16),
            pltpu.VMEM((TERMS - 1, pixels_f, half), F32),
            [pltpu.VMEM((n_f, B, half), BF16)] * 3,
            [pltpu.VMEM((3 * RIM_F, B, half), BF16)] * 3,
            [pltpu.VMEM((3 * RIM_F, B, half), BF16)] * 3,
            dma((6,)),
            dma((2,)),
            dma((5, 2)),
            dma((steps, 2)),
            dma((3, 2, 2)),
            dma((3, 2, 2)),
        ],
        compiler_params=pltpu.CompilerParams(
            collective_id=0, has_side_effects=True, vmem_limit_bytes=60 * 1024 * 1024
        ),
    )(
        coarse_map,
        skip_map,
        coarse_values.T,
        coarse_columns.T,
        fine_values.T,
        fine_columns.T,
        coarse_weight,
        coarse_bias.reshape(1, half),
        up_weight,
        skip_weight,
        fine_bias.reshape(1, half),
    )


def solution(mesh):
    placed = (
        P("patch", "chan"),
        P("patch", "chan"),
        P("patch", None),
        P("patch", None),
        P("patch", None),
        P("patch", None),
        P(None, "chan", None),
        P("chan"),
        P(None, "chan", None),
        P(None, "chan", None),
        P("chan"),
    )
    return jax.shard_map(
        functools.partial(per_device, mesh.shape["patch"]),
        mesh=mesh,
        in_specs=placed,
        out_specs=P("patch", "chan"),
        check_vma=False,
    )
```

```python
import functools

import jax
import jax.numpy as jnp
from jax import lax
from jax.experimental import pallas as pl
from jax.experimental.pallas import tpu as pltpu
from jax.sharding import PartitionSpec as P

B = 64
NB = 9
RIM_C = 8
RIM_F = 16
TERMS = 4
FLIP = 8
F32 = jnp.float32
BF16 = jnp.bfloat16
MESH = pl.DeviceIdType.MESH


def dot(a, b):
    return jnp.dot(a, b, preferred_element_type=F32)


def place_of(offset, blocks_all, held):
    return jnp.minimum(lax.bitwise_and(offset, blocks_all - 1), held - 1)


def kernel(
    n_patch,
    cm,
    skip,
    vc_hbm,
    jc,
    vf_hbm,
    jf,
    wc_hbm,
    cb_hbm,
    up_hbm,
    sw_hbm,
    fb,
    out,
    cm_own,
    cm_oth,
    vc,
    wc,
    cb,
    up,
    sw,
    skip_own,
    skip_oth,
    vf,
    turned,
    coarse_own,
    coarse_lo,
    coarse_hi,
    gc,
    hidden,
    g,
    fine_own,
    fine_lo,
    fine_hi,
    load_sem,
    turn_sem,
    gather_sem,
    skip_sem,
    halo_c_sem,
    halo_f_sem,
):
    p = lax.axis_index("patch")
    c = lax.axis_index("chan")
    left = (lax.rem(p + n_patch - 1, n_patch), c)
    right = (lax.rem(p + 1, n_patch), c)
    partner = (p, 1 - c)
    row = lax.rem(p, FLIP)
    coarse_left = (left[0], jnp.where(row == 0, 1 - c, c))
    coarse_right = (right[0], jnp.where(row == FLIP - 1, 1 - c, c))
    z_hi = lax.rem(p // FLIP, 2)
    far = (p + FLIP - 2 * FLIP * z_hi, 1 - c)

    n_c = vc.shape[0]
    n_f = vf.shape[0]
    all_c = n_c * n_patch
    all_f = n_f * n_patch
    half = cm.shape[1]
    full = 2 * half

    def remote(src, dst, sems, target):
        return pltpu.make_async_remote_copy(
            src_ref=src,
            dst_ref=dst,
            send_sem=sems.at[0],
            recv_sem=sems.at[1],
            device_id=target,
            device_id_type=MESH,
        )

    own_rows = pl.ds(pl.multiple_of(c * half, half), half)
    own_cols = own_rows
    far_cols = pl.ds(pl.multiple_of((1 - c) * half, half), half)

    lanes = 128
    cols = turned.shape[2]
    c_parts = n_c * B // cols
    f_parts = n_f * B // cols

    def entries(source, i, slot):
        part = pl.ds(pl.multiple_of(i * cols, cols), cols)
        return pltpu.make_async_copy(source.at[:, part], turned.at[slot], turn_sem.at[slot])

    def turn(target, i, slot):
        for t in range(cols // lanes):
            value = turned[slot, :, t * lanes : (t + 1) * lanes].T
            blocks = pl.ds(i * (cols // B) + t * (lanes // B), lanes // B)
            target[blocks] = value.reshape(lanes // B, B, value.shape[1])

    def turn_coarse():
        for i in range(c_parts):
            slot = i % 2
            entries(vc_hbm, i, slot).wait()
            turn(vc, i, slot)
            if i + 2 < c_parts:
                entries(vc_hbm, i + 2, slot).start()
            else:
                entries(vf_hbm, i + 2 - c_parts, slot).start()

    def turn_fine(start, stop):
        @pl.loop(start // 2, stop // 2)
        def _(pair):
            for slot in range(2):
                i = 2 * pair + slot
                entries(vf_hbm, i, slot).wait()
                turn(vf, i, slot)

                @pl.when(i + 2 < f_parts)
                def _():
                    entries(vf_hbm, i + 2, slot).start()

    pairs = [
        (cm, cm_own),
        (wc_hbm, wc.at[:, pl.ds(0, half), :]),
        (cb_hbm, cb.at[c]),
        (up_hbm.at[:, :, own_cols], up.at[:, own_rows, :]),
        (sw_hbm.at[:, :, own_cols], sw.at[:, pl.ds(0, half), :]),
        (skip, skip_own),
    ]
    loads = [pltpu.make_async_copy(a, b, load_sem.at[i]) for i, (a, b) in enumerate(pairs)]
    entries(vc_hbm, 0, 0).start()
    entries(vc_hbm, 1, 1).start()
    for load in loads:
        load.start()

    barrier = pltpu.get_barrier_semaphore()
    for target in (left, right, coarse_left, coarse_right, partner, far):
        pl.semaphore_signal(barrier, inc=1, device_id=target, device_id_type=MESH)
    pl.semaphore_wait(barrier, 6)

    cm_copy = remote(cm, cm_oth, gather_sem.at[0], partner)
    wc_copy = remote(wc_hbm, wc.at[:, pl.ds(half, half), :], gather_sem.at[1], far)
    cb_copy = remote(cb_hbm, cb.at[c], gather_sem.at[2], far)
    up_copy = remote(up_hbm.at[:, :, far_cols], up.at[:, own_rows, :], gather_sem.at[3], far)
    sw_copy = remote(
        sw_hbm.at[:, :, far_cols], sw.at[:, pl.ds(half, half), :], gather_sem.at[4], far
    )
    gathers = [cm_copy, wc_copy, cb_copy, up_copy, sw_copy]
    for copy in gathers:
        copy.start()

    chunk = 8
    steps = n_f // chunk
    rows = chunk * B

    def skip_copy(q):
        part = pl.ds(pl.multiple_of(q * rows, rows), rows)
        return remote(skip.at[part], skip_oth.at[part], skip_sem.at[q], partner)

    def skip_send(*pair_numbers):
        for q in pair_numbers:
            skip_copy(q).start()
            skip_copy(steps - 1 - q).start()

    skip_send(0)
    for load in loads[:3]:
        load.wait()
    turn_coarse()
    for copy in (wc_copy, cb_copy, cm_copy):
        copy.wait_recv()
    cm_copy.wait_send()

    skip_send(1, 2)

    def coarse_keep(slot, r, values):
        coarse_own[slot][r] = values
        if r < n_c // 2:
            coarse_lo[slot][RIM_C + r] = values
        else:
            coarse_hi[slot][r - n_c // 2] = values

    def coarse_g(first, count, k):
        part = pl.ds(first * B, count * B)
        x = jnp.concatenate([cm_own[part, :], cm_oth[part, :]], axis=1)
        return dot(x, wc[k])

    def coarse_halo(slot):
        sems = halo_c_sem.at[slot]
        to_left = remote(
            coarse_lo[slot].at[pl.ds(RIM_C, RIM_C)],
            coarse_hi[slot].at[pl.ds(n_c // 2, RIM_C)],
            sems.at[0],
            coarse_left,
        )
        to_right = remote(
            coarse_hi[slot].at[pl.ds(n_c // 2 - RIM_C, RIM_C)],
            coarse_lo[slot].at[pl.ds(0, RIM_C)],
            sems.at[1],
            coarse_right,
        )
        return to_left, to_right

    def coarse_first(first):
        values = coarse_g(first, RIM_C, 3).astype(BF16).reshape(RIM_C, B, full)
        for i in range(RIM_C):
            coarse_keep(0, first + i, values[i])

    coarse_first(0)
    coarse_first(n_c - RIM_C)
    halos = [coarse_halo(0)]
    for copy in halos[-1]:
        copy.start()
    for first in range(RIM_C, n_c - RIM_C, RIM_C):
        coarse_first(first)

    @pl.loop(0, n_c // RIM_C)
    def _(q):
        part = pl.ds(pl.multiple_of(q * RIM_C * B, RIM_C * B), RIM_C * B)
        x = jnp.concatenate([cm_own[part, :], cm_oth[part, :]], axis=1)
        for k in range(TERMS - 1):
            value = dot(x, wc[k])
            gc[2 * k, part, :] = value[:, :half]
            gc[2 * k + 1, part, :] = value[:, half:]

    skip_send(3)
    bias_c = jnp.concatenate([cb[0], cb[1]], axis=1)

    def coarse_rows(slot, numbers):
        k = 2 - slot
        for r in numbers:
            if r < RIM_C:
                source, first = coarse_lo, -RIM_C
            elif r >= n_c - RIM_C:
                source, first = coarse_hi, n_c // 2
            else:
                source, first = coarse_own, 0
            base = p * n_c + first
            picked = [
                source[slot][place_of(jc[j, r] - base, all_c, source[slot].shape[0])] for j in range(NB)
            ]
            value = dot(vc[r], jnp.concatenate(picked, axis=0))
            part = pl.ds(r * B, B)
            term = jnp.concatenate([gc[2 * k, part, :], gc[2 * k + 1, part, :]], axis=1)
            if k > 0:
                value = 2.0 * value
            value = term + value
            if slot > 0:
                value = value - coarse_own[slot - 1][r].astype(F32)
            if k > 0:
                coarse_keep(slot + 1, r, value.astype(BF16))
            else:
                hidden[r] = jnp.maximum(value + bias_c, 0.0).astype(BF16)

    for slot in range(3):
        coarse_rows(slot, range(RIM_C, n_c - RIM_C))
        skip_send(4 + slot)
        turn_fine(slot * (f_parts // 4), (slot + 1) * (f_parts // 4))
        for copy in halos[-1]:
            copy.wait_recv()
        coarse_rows(slot, [*range(RIM_C), *range(n_c - RIM_C, n_c)])
        if slot < 2:
            halos.append(coarse_halo(slot + 1))
            for copy in halos[-1]:
                copy.start()

    for load in loads[3:]:
        load.wait()
    up_copy.wait_recv()
    sw_copy.wait_recv()
    quarter = gc.shape[1]

    @pl.loop(0, n_c // 4)
    def _(q):
        count = 4 * B
        x = hidden[pl.ds(q * 4, 4)].reshape(count, full)
        low = dot(x, jnp.concatenate([up[0], up[1]], axis=1))
        high = dot(x, jnp.concatenate([up[2], up[3]], axis=1))
        slot = 2 + (4 * count * q) // quarter
        start = (4 * count * q) % quarter
        for i in range(4):
            part = pl.ds(4 * count * q + i, count, stride=4)
            g[0, part, :] = low[:, :half] + fb[...]
            g[1, part, :] = low[:, half:]
            g[2, part, :] = high[:, :half]
            gc[slot, pl.ds(start + i, count, stride=4), :] = high[:, half:]

    skip_send(7)
    turn_fine(3 * (f_parts // 4), f_parts)

    edge = RIM_F // chunk
    ends = 2 * edge

    def fine_keep(slot, near, i, r, values):
        fine_own[slot][r] = values
        if near == "lo":
            fine_lo[slot][RIM_F + r] = values
        if near == "hi":
            fine_hi[slot][r - (n_f - 2 * RIM_F)] = values

    def both(q, near):
        return ((q, "lo" if near else None), (steps - 1 - q, "hi" if near else None))

    def fine_first(q, near):
        for at, side in both(q, near):
            skip_copy(at).wait_recv()
        for at, side in both(q, near):
            part = pl.ds(pl.multiple_of(at * rows, rows), rows)
            x = jnp.concatenate([skip_own[part, :], skip_oth[part, :]], axis=1)
            low = dot(x, jnp.concatenate([sw[0], sw[1]], axis=1))
            high = dot(x, jnp.concatenate([sw[2], sw[3]], axis=1))
            g[0, part, :] += low[:, :half]
            g[1, part, :] += low[:, half:]
            g[2, part, :] += high[:, :half]
            slot = 2 + (at * rows) // quarter
            start = pl.multiple_of((at * rows) % quarter, rows)
            value = high[:, half:] + gc[slot, pl.ds(start, rows), :]
            value = value.astype(BF16).reshape(chunk, B, half)
            for i in range(chunk):
                fine_keep(0, side, i, at * chunk + i, value[i])

    def fine_halo(slot):
        sems = halo_f_sem.at[slot]
        to_left = remote(
            fine_lo[slot].at[pl.ds(RIM_F, RIM_F)],
            fine_hi[slot].at[pl.ds(2 * RIM_F, RIM_F)],
            sems.at[0],
            left,
        )
        to_right = remote(
            fine_hi[slot].at[pl.ds(RIM_F, RIM_F)],
            fine_lo[slot].at[pl.ds(0, RIM_F)],
            sems.at[1],
            right,
        )
        return to_left, to_right

    def fine_rows(slot, q, near, border=False):
        k = 2 - slot
        for at, side in both(q, near):
            if not border:
                source, first = fine_own, 0
            elif side == "lo":
                source, first = fine_lo, -RIM_F
            else:
                source, first = fine_hi, n_f - 2 * RIM_F
            base = p * n_f + first
            for i in range(chunk):
                r = at * chunk + i
                part = pl.ds(pl.multiple_of(r * B, B), B)
                picked = [
                    source[slot][place_of(jf[j, r] - base, all_f, source[slot].shape[0])]
                    for j in range(NB)
                ]
                value = dot(vf[r], jnp.concatenate(picked, axis=0))
                if k > 0:
                    value = 2.0 * value
                value = g[k, part, :] + value
                if slot > 0:
                    value = value - fine_own[slot - 1][r].astype(F32)
                value = value.astype(BF16)
                if k > 0:
                    fine_keep(slot + 1, side, i, r, value)
                else:
                    out[part, :] = value

    fine_halos = []

    def send(slot):
        fine_halos.append(fine_halo(slot))
        for copy in fine_halos[-1]:
            copy.start()

    def arrived(slot):
        for copy in fine_halos[slot]:
            copy.wait_recv()

    def run(start, stop, body):
        if stop - start == 1:
            body(start)
        else:
            pl.loop(start, stop)(body)

    def first_of(start, stop, near):
        run(start, stop, lambda q: fine_first(q, near))

    def rows_of(slot, start, stop, near, border=False):
        run(start, stop, lambda q: fine_rows(slot, q, near, border))

    middle = steps // 2
    first_of(0, edge, True)
    send(0)
    first_of(edge, ends, True)
    first_of(ends, ends + 2, False)
    rows_of(0, edge, ends, True)
    arrived(0)
    rows_of(0, 0, edge, True, True)
    send(1)
    first_of(ends + 2, ends + 3, False)
    rows_of(0, ends, ends + 1, False)
    rows_of(1, edge, edge + 1, True)
    arrived(1)
    rows_of(1, 0, edge, True, True)
    send(2)
    first_of(ends + 3, middle, False)
    rows_of(0, ends + 1, middle, False)
    rows_of(1, edge + 1, ends, True)
    rows_of(1, ends, middle, False)
    rows_of(2, edge, middle, False)
    arrived(2)
    rows_of(2, 0, edge, True, True)

    @pl.loop(0, steps)
    def _(q):
        skip_copy(q).wait_send()

    for pair in halos + fine_halos:
        for copy in pair:
            copy.wait_send()
    for copy in gathers[1:]:
        copy.wait_send()


def per_device(
    n_patch,
    coarse_map,
    skip_map,
    coarse_values,
    coarse_columns,
    fine_values,
    fine_columns,
    coarse_weight,
    coarse_bias,
    up_weight,
    skip_weight,
    fine_bias,
):
    pixels_c, half = coarse_map.shape
    pixels_f = skip_map.shape[0]
    width = coarse_values.shape[1]
    n_c, n_f = pixels_c // B, pixels_f // B
    full = 2 * half
    steps = n_f // 8
    anywhere = pl.BlockSpec(memory_space=pl.ANY)
    scalars = pl.BlockSpec(memory_space=pltpu.SMEM)
    vmem = pl.BlockSpec(memory_space=pltpu.VMEM)
    dma = pltpu.SemaphoreType.DMA
    return pl.pallas_call(
        functools.partial(kernel, n_patch),
        out_shape=pltpu.VMEM((pixels_f, half), BF16),
        in_specs=[
            anywhere,
            anywhere,
            anywhere,
            scalars,
            anywhere,
            scalars,
            anywhere,
            anywhere,
            anywhere,
            anywhere,
            vmem,
        ],
        out_specs=vmem,
        scratch_shapes=[
            pltpu.VMEM((pixels_c, half), BF16),
            pltpu.VMEM((pixels_c, half), BF16),
            pltpu.VMEM((n_c, B, width), BF16),
            pltpu.VMEM((TERMS, full, full), BF16),
            pltpu.VMEM((2, 1, half), F32),
            pltpu.VMEM((TERMS, full, half), BF16),
            pltpu.VMEM((TERMS, full, half), BF16),
            pltpu.VMEM((pixels_f, half), BF16),
            pltpu.VMEM((pixels_f, half), BF16),
            pltpu.VMEM((n_f, B, width), BF16),
            pltpu.VMEM((2, width, 512), BF16),
            [pltpu.VMEM((n_c, B, full), BF16)] * 3,
            [pltpu.VMEM((n_c // 2 + RIM_C, B, full), BF16)] * 3,
            [pltpu.VMEM((n_c // 2 + RIM_C, B, full), BF16)] * 3,
            pltpu.VMEM((2 * (TERMS - 1), pixels_c, half), F32),
            pltpu.VMEM((n_c, B, full), BF16),
            pltpu.VMEM((TERMS - 1, pixels_f, half), F32),
            [pltpu.VMEM((n_f, B, half), BF16)] * 3,
            [pltpu.VMEM((3 * RIM_F, B, half), BF16)] * 3,
            [pltpu.VMEM((3 * RIM_F, B, half), BF16)] * 3,
            dma((6,)),
            dma((2,)),
            dma((5, 2)),
            dma((steps, 2)),
            dma((3, 2, 2)),
            dma((3, 2, 2)),
        ],
        compiler_params=pltpu.CompilerParams(
            collective_id=0, has_side_effects=True, vmem_limit_bytes=60 * 1024 * 1024
        ),
    )(
        coarse_map,
        skip_map,
        coarse_values.T,
        coarse_columns.T,
        fine_values.T,
        fine_columns.T,
        coarse_weight,
        coarse_bias.reshape(1, half),
        up_weight,
        skip_weight,
        fine_bias.reshape(1, half),
    )


def solution(mesh):
    placed = (
        P("patch", "chan"),
        P("patch", "chan"),
        P("patch", None),
        P("patch", None),
        P("patch", None),
        P("patch", None),
        P(None, "chan", None),
        P("chan"),
        P(None, "chan", None),
        P(None, "chan", None),
        P("chan"),
    )
    return jax.shard_map(
        functools.partial(per_device, mesh.shape["patch"]),
        mesh=mesh,
        in_specs=placed,
        out_specs=P("patch", "chan"),
        check_vma=False,
    )
```
